128 devices in a mesh: row: 16 (over y, x), col: 8 (over z, core).
Axes of the slice: x: 4, y: 4, z: 4, core: 2. Of those that a mesh axis runs over, the one named last changes fastest.
Arguments:
- activations: bfloat16 [4096, 8192], P('row', 'col'), may hold values from -6 to 6
- out_grads: bfloat16 [4096, 8192], P('col', 'row'), may hold values from -6 to 6
- input_basis: bfloat16 [8192, 8192], P('col', 'row'), may hold values from -0.0625 to 0.0625
- output_basis: bfloat16 [8192, 8192], P('row', 'col'), may hold values from -0.0625 to 0.0625
Outputs:
- correction: float32 [8192, 8192], P('row', 'col')
The draws below stay inside these ranges and needn't reach their ends.
All inputs are finite; a program needn't handle non-finite values.
Results may differ from the reference program's by a relative error of at most 0.02.
Values may be sent and summed in bfloat16 or wider, within the bound.
A program may use at most 128 MiB of HBM per device.

```python
import jax
import jax.numpy as jnp
from jax import lax

D = 8192
SEQS = 4
SEQ_LEN = 1024
TOKENS = 4096
N_ROW = 16
N_COL = 8


def level_of(stream_key, extent, pieces, low, top_value):
    def one(dim, shards_of):
        draws = jax.random.uniform(jax.random.fold_in(jax.random.fold_in(stream_key, 6), dim), (shards_of,), jnp.float32, low / len(pieces), top_value / len(pieces))
        return jnp.repeat(jnp.exp(draws), extent[dim] // shards_of).reshape((-1,) + (1,) * (len(extent) - dim - 1))

    loudness = one(*pieces[0])
    for cut in pieces[1:]:
        loudness = loudness * one(*cut)
    return loudness


def bell_draw(own_key, dims, spread, limit, shards=(), held_as=jnp.bfloat16):
    array = spread * jax.random.normal(own_key, dims, jnp.float32)
    if shards:
        array = array * level_of(own_key, dims, shards, -0.22, 0.18)
    return jnp.clip(array, -limit, limit).astype(held_as)


def setup_inputs(seed: int = 0) -> dict:
    key_of = jax.random.split(jax.random.key(seed), 5)
    activations = bell_draw(key_of[0], (TOKENS, D), 1.0, 6.0, ((0, 16), (1, 8)))
    out_grads = bell_draw(key_of[1], (TOKENS, D), 1.0, 6.0, ((0, 8), (1, 16)))
    input_basis = bell_draw(key_of[2], (D, D), D ** -0.5, 0.0625, ((0, 8), (1, 16)))
    output_basis = bell_draw(key_of[3], (D, D), D ** -0.5, 0.0625, ((0, 16), (1, 8)))
    return dict(activations=activations, out_grads=out_grads, input_basis=input_basis, output_basis=output_basis)


def rotate_blocks(data, basis, count):
    block_width = D // count
    total = jnp.zeros((data.shape[0], basis.shape[1]), jnp.float32)
    for part_index in range(count):
        lower = part_index * block_width
        term = jnp.dot(data[:, lower:lower + block_width], basis[lower:lower + block_width, :], preferred_element_type=jnp.float32)
        rounded = lax.optimization_barrier(term.astype(jnp.bfloat16))
        total = total + rounded.astype(jnp.float32)
    return total.astype(jnp.bfloat16)


def reference(activations, out_grads, input_basis, output_basis):
    act_rot = rotate_blocks(activations, input_basis, N_COL)
    grad_rot = rotate_blocks(out_grads, output_basis, N_ROW)
    result = jnp.zeros((D, D), jnp.float32)
    for seq_index in range(SEQS):
        lower = seq_index * SEQ_LEN
        act_seq = act_rot[lower:lower + SEQ_LEN].astype(jnp.float32)
        grad_seq = grad_rot[lower:lower + SEQ_LEN].astype(jnp.float32)
        tile = jnp.einsum("ti,tj->ij", act_seq, grad_seq)
        result = result + tile * tile
    return result / (SEQS * SEQ_LEN)
```

```python
import functools

import jax
import jax.numpy as jnp
from jax import lax
from jax.experimental import pallas as pl
from jax.experimental.pallas import tpu as pltpu
from jax.sharding import PartitionSpec as P

SEQS = 4
SEQ_LEN = 1024
MESH = pl.DeviceIdType.MESH
BF16 = jnp.bfloat16
F32 = jnp.float32
N_SEM = 200


def at_multiple(index, size, step=None):
    return pl.ds(pl.multiple_of(index * (step or size), step or size), size)


def kernel(
    a_ref, g_ref, u_ref, v_ref, o_ref,
    a_all, u_all, g_all, v_all,
    act_out, act_in, act_part, act_s1, act_r1, act_s2, act_r2, act_t,
    grad_part, grad_s1, grad_r1, grad_s2, grad_r2, grad_rot,
    tile_part, tile_s1, tile_r1, tile_s2, tile_r2,
    send_sem, recv_sem, local_sem,
):
    row, col = lax.axis_index("row"), lax.axis_index("col")
    y, x = lax.div(row, 4), lax.rem(row, 4)
    z, core = lax.div(col, 2), lax.rem(col, 2)
    mate = 1 - core

    def step(position, by):
        return lax.rem(position + by, 4)

    def device(y, x, z, core):
        return (y * 4 + x, z * 2 + core)

    x_ring = (device(y, step(x, 1), z, core), device(y, step(x, 3), z, core))
    y_ring = (device(step(y, 1), x, z, core), device(step(y, 3), x, z, core))
    z_ring = (device(y, x, step(z, 1), core), device(y, x, step(z, 3), core))
    x_far = device(y, step(x, 2), z, core)
    other = device(y, x, z, mate)

    partners = (*x_ring, *y_ring, *z_ring, x_far, other)
    barrier = pltpu.get_barrier_semaphore()
    for partner in partners:
        pl.semaphore_signal(barrier, inc=1, device_id=partner, device_id_type=MESH)
    pl.semaphore_wait(barrier, len(partners))

    sent = []

    def send(src, dst, target):
        index = len(sent)
        copy = pltpu.make_async_remote_copy(
            src_ref=src, dst_ref=dst,
            send_sem=send_sem.at[index], recv_sem=recv_sem.at[index],
            device_id=target, device_id_type=MESH,
        )
        copy.start()
        sent.append(copy)
        return copy

    local = []

    def keep(src, dst):
        copy = pltpu.make_async_copy(src, dst, local_sem.at[len(local)])
        copy.start()
        local.append(copy)
        return copy

    class Gather:
        def __init__(self, slot, position, ring, own=None):
            own = own or (lambda half: slot(position, half))
            self.slot, self.position, self.ring = slot, position, ring
            right, left = ring
            self.r0 = send(own(0), slot(position, 0), right)
            self.l1 = send(own(1), slot(position, 1), left)
            self.r1 = send(own(1), slot(position, 1), right)
            self.l0 = send(own(0), slot(position, 0), left)

        def forward(self):
            right, left = self.ring
            self.r0.wait_recv()
            before = self.slot(step(self.position, 3), 0)
            self.rr = send(before, before, right)
            self.l1.wait_recv()
            after = self.slot(step(self.position, 1), 1)
            self.ll = send(after, after, left)

        def near(self):
            self.r1.wait_recv()
            self.l0.wait_recv()

        def far(self):
            self.rr.wait_recv()
            self.ll.wait_recv()

    class Reduce:
        def __init__(self, part, half, position, ring, s1, r1, s2, r2):
            self.part, self.half, self.position, self.ring = part, half, position, ring
            self.s1, self.r1, self.s2, self.r2 = s1, r1, s2, r2

        def first(self):
            right, left = self.ring
            block = self.part(step(self.position, 2))
            self.s1[0] = block[:self.half].astype(BF16)
            self.s1[1] = block[self.half:].astype(BF16)
            self.right1 = send(self.s1.at[0], self.r1.at[0], right)
            self.left1 = send(self.s1.at[1], self.r1.at[1], left)

        def second(self):
            right, left = self.ring
            half = self.half
            block = self.part(step(self.position, 1))
            self.right1.wait_recv()
            self.s2[0, :half] = (block[:half] + self.r1[0].astype(F32)).astype(BF16)
            self.s2[0, half:] = block[half:].astype(BF16)
            self.right2 = send(self.s2.at[0], self.r2.at[0], right)
            block = self.part(step(self.position, 3))
            self.left1.wait_recv()
            self.s2[1, :half] = block[:half].astype(BF16)
            self.s2[1, half:] = (block[half:] + self.r1[1].astype(F32)).astype(BF16)
            self.left2 = send(self.s2.at[1], self.r2.at[1], left)

        def last(self):
            block = self.part(self.position)
            self.right2.wait_recv()
            self.left2.wait_recv()
            return block + self.r2[0].astype(F32) + self.r2[1].astype(F32)

    own_rows = pl.multiple_of(z * 256 + core * 128, 128)
    lanes = at_multiple(x, 512)
    swaps = []
    for by, target in ((1, x_ring[0]), (3, x_ring[1]), (2, x_far)):
        swaps.append(send(
            g_ref.at[at_multiple(step(x, by), 128)],
            g_all.at[pl.ds(own_rows, 128), lanes], target))
    g_own = keep(g_ref.at[at_multiple(x, 128)], g_all.at[pl.ds(own_rows, 128), lanes])

    u_gather = Gather(
        lambda p, half: u_all.at[p * 2 + half], y, y_ring,
        own=lambda half: u_ref.at[:, pl.ds(half * 256, 256)])
    a_gather = Gather(
        lambda p, half: a_all.at[pl.ds(pl.multiple_of(p * 256 + half * 128, 128), 128)], x, x_ring,
        own=lambda half: a_ref.at[pl.ds(half * 128, 128)])
    keeps = [
        keep(a_ref, a_all.at[at_multiple(x, 256)]),
        keep(u_ref.at[:, pl.ds(0, 256)], u_all.at[y * 2]),
        keep(u_ref.at[:, pl.ds(256, 256)], u_all.at[y * 2 + 1]),
    ]
    for c in range(4):
        keeps.append(keep(v_ref.at[:, pl.ds(c * 256, 256)], v_all.at[c, at_multiple(x, 512)]))

    def v_start(c):
        return Gather(
            lambda p, half: v_all.at[c, pl.ds(pl.multiple_of(p * 512 + half * 256, 256), 256)], x, x_ring,
            own=lambda half: v_ref.at[pl.ds(half * 256, 256), pl.ds(c * 256, 256)])

    g_own.wait()
    for swap in swaps:
        swap.wait_recv()

    def g_rows(p, owner):
        return g_all.at[pl.ds(pl.multiple_of(p * 256 + owner * 128, 128), 128)]

    g_gather = Gather(
        lambda p, half: g_all.at[pl.ds(pl.multiple_of(p * 256 + core * 128 + half * 64, 64), 64)], z, z_ring)
    g_mates = [send(g_rows(z, core), g_rows(z, core), other)]

    a_gather.forward()
    v_gathers = [v_start(0)]
    g_gather.forward()
    u_gather.forward()
    v_gathers.append(v_start(1))
    for copy in keeps:
        copy.wait()
    a_gather.near()
    a_gather.far()

    def dot(a, b):
        return jnp.dot(a, b, preferred_element_type=F32)

    act_pieces = []

    class Piece:
        def __init__(self, s, block):
            self.s, self.block = s, block

            @pl.loop(0, 2)
            def _(m):
                rows = at_multiple(m, 512)
                act_out[s, rows] = dot(a_all[rows], u_all[block * 2 + mate]).astype(BF16)

            self.swap = send(act_out.at[s], act_in.at[s], other)

            @pl.loop(0, 2)
            def _(m):
                rows = at_multiple(m, 512)
                act_part[s, rows] = dot(a_all[rows], u_all[block * 2 + core])

            def part(t):
                rows = at_multiple(t, 256)
                return act_part[s, rows] + act_in[s, rows].astype(F32)

            self.reduce = Reduce(part, 128, z, z_ring, act_s1.at[s], act_r1.at[s], act_s2.at[s], act_r2.at[s])
            self.swap.wait_recv()
            self.reduce.first()

        def gather(self):
            total = self.reduce.last()
            rows = pl.multiple_of(self.block * 512 + core * 256, 256)
            act_t[pl.ds(rows, 256), at_multiple(z, 256)] = total.T.astype(BF16)
            self.gathered = Gather(
                lambda p, half: act_t.at[pl.ds(pl.multiple_of(rows + half * 128, 128), 128), at_multiple(p, 256)],
                z, z_ring)

        def finish(self):
            self.gathered.near()
            self.gathered.far()
            rows = pl.multiple_of(self.block * 512 + core * 256, 256)
            piece = act_t.at[pl.ds(rows, 256)]
            self.mate = send(piece, piece, other)

    class Chunk:
        def __init__(self, c):
            self.c = c

            @pl.loop(0, 2)
            def _(m):
                rows = at_multiple(m, 512)
                grad_part[c, rows] = dot(g_all[rows], v_all[c])

            def part(t):
                return grad_part[c, at_multiple(t, 256)]

            self.reduce = Reduce(part, 128, y, y_ring, grad_s1.at[c], grad_r1.at[c], grad_s2.at[c], grad_r2.at[c])
            self.reduce.first()

        def gather(self):
            c = self.c
            total = self.reduce.last().astype(BF16)
            rows = at_multiple(x, 128)
            grad_rot[c, 0, rows] = total[:128]
            grad_rot[c, 1, rows] = total[128:]
            self.gathered = Gather(
                lambda p, half: grad_rot.at[c, half, at_multiple(p, 128)], x, x_ring)

        def finish(self):
            self.gathered.near()
            self.gathered.far()

        def tiles(self):
            c = self.c
            grads = grad_rot[c].reshape(1024, 256)

            def tile(t):
                product = dot(act_t[at_multiple(t, 512)], grads)
                return product * product

            def part(t):
                return tile(t)

            self.out = Reduce(part, 256, y, y_ring, tile_s1.at[c], tile_r1.at[c], tile_s2.at[c], tile_r2.at[c])
            self.out.first()

        def total(self):
            o_ref[:, pl.ds(self.c * 256, 256)] = self.out.last() * (1.0 / (SEQS * SEQ_LEN))

    pieces = [Piece(0, y)]
    u_gather.near()
    v_gathers[0].forward()
    g_gather.near()
    for by in (1, 3):
        g_mates.append(send(g_rows(step(z, by), core), g_rows(step(z, by), core), other))
    v_gathers.append(v_start(2))
    pieces.append(Piece(1, step(y, 3)))
    pieces[0].reduce.second()
    pieces.append(Piece(2, step(y, 1)))
    pieces[1].reduce.second()
    v_gathers[1].forward()
    g_gather.far()
    g_mates.append(send(g_rows(step(z, 2), core), g_rows(step(z, 2), core), other))
    v_gathers.append(v_start(3))
    pieces[2].reduce.second()
    pieces[0].gather()
    for copy in g_mates:
        copy.wait_recv()
    chunks = []
    v_gathers[0].near()
    v_gathers[0].far()
    chunks.append(Chunk(0))
    u_gather.far()
    pieces.append(Piece(3, step(y, 2)))
    pieces[0].gathered.forward()
    pieces[1].gather()
    chunks[0].reduce.second()
    pieces[3].reduce.second()
    v_gathers[2].forward()
    pieces[1].gathered.forward()
    pieces[2].gather()
    v_gathers[1].near()
    v_gathers[1].far()
    chunks.append(Chunk(1))
    chunks[0].gather()
    pieces[0].finish()
    pieces[2].gathered.forward()
    pieces[3].gather()
    chunks[1].reduce.second()
    chunks[0].gathered.forward()
    v_gathers[3].forward()
    pieces[1].finish()
    pieces[3].gathered.forward()
    v_gathers[2].near()
    v_gathers[2].far()
    chunks.append(Chunk(2))
    chunks[1].gather()
    pieces[2].finish()
    chunks[2].reduce.second()
    chunks[1].gathered.forward()
    v_gathers[3].near()
    v_gathers[3].far()
    chunks.append(Chunk(3))
    chunks[2].gather()
    pieces[3].finish()
    chunks[3].reduce.second()
    for piece in pieces:
        piece.mate.wait_recv()
    chunks[0].finish()
    chunks[0].tiles()
    chunks[2].gathered.forward()
    chunks[3].gather()
    chunks[1].finish()
    chunks[1].tiles()
    chunks[0].out.second()
    chunks[3].gathered.forward()
    chunks[2].finish()
    chunks[2].tiles()
    chunks[1].out.second()
    chunks[3].finish()
    chunks[3].tiles()
    chunks[2].out.second()
    chunks[0].total()
    chunks[3].out.second()
    chunks[1].total()
    chunks[2].total()
    chunks[3].total()
    for copy in sent:
        copy.wait_send()


def shards(activations, out_grads, input_basis, output_basis):
    vmem = pl.BlockSpec(memory_space=pltpu.VMEM)
    bf16_sizes = lambda *s: pltpu.VMEM(s, BF16)
    f32_sizes = lambda *s: pltpu.VMEM(s, F32)
    return pl.pallas_call(
        kernel,
        out_shape=jax.ShapeDtypeStruct((512, 1024), F32),
        in_specs=[vmem] * 4,
        out_specs=vmem,
        scratch_shapes=[
            bf16_sizes(1024, 1024), bf16_sizes(8, 1024, 256), bf16_sizes(1024, 2048), bf16_sizes(4, 2048, 256),
            bf16_sizes(4, 1024, 256), bf16_sizes(4, 1024, 256), f32_sizes(4, 1024, 256),
            bf16_sizes(4, 2, 128, 256), bf16_sizes(4, 2, 128, 256),
            bf16_sizes(4, 2, 256, 256), bf16_sizes(4, 2, 256, 256), bf16_sizes(2048, 1024),
            f32_sizes(4, 1024, 256),
            bf16_sizes(4, 2, 128, 256), bf16_sizes(4, 2, 128, 256),
            bf16_sizes(4, 2, 256, 256), bf16_sizes(4, 2, 256, 256), bf16_sizes(4, 2, 512, 256),
            f32_sizes(8, 128),
            bf16_sizes(4, 2, 256, 256), bf16_sizes(4, 2, 256, 256),
            bf16_sizes(4, 2, 512, 256), bf16_sizes(4, 2, 512, 256),
            pltpu.SemaphoreType.DMA((N_SEM,)), pltpu.SemaphoreType.DMA((N_SEM,)),
            pltpu.SemaphoreType.DMA((16,)),
        ],
        compiler_params=pltpu.CompilerParams(
            collective_id=0, has_side_effects=True, vmem_limit_bytes=60 * 2**20),
        cost_estimate=pl.CostEstimate(flops=13 * 10**9, bytes_accessed=5 * 2**20, transcendentals=0),
    )(activations, out_grads, input_basis, output_basis)


def solution(mesh):
    return jax.shard_map(
        shards,
        mesh=mesh,
        in_specs=(P("row", "col"), P("col", "row"), P("col", "row"), P("row", "col")),
        out_specs=P("row", "col"),
        check_vma=False,
    )
```

```python
import jax
import jax.numpy as jnp
from jax import lax
from jax.experimental import pallas as pl
from jax.experimental.pallas import tpu as pltpu
from jax.sharding import PartitionSpec as P

SEQS = 4
SEQ_LEN = 1024
MESH = pl.DeviceIdType.MESH
BF16 = jnp.bfloat16
F32 = jnp.float32
CHUNKS = 4
WIDTH = 1024 // CHUNKS
N_SEM = 120 + 24 * CHUNKS

ORDER = (
    "ga", "a.own1", "a.own2", "u.own1", "gk.own", "g.own1", "u.fwd", "a.fwd", "g.fwd", "v1.own1", "u.own2",
    "v2.own1", "g.own2", "v1.own2", "p1.own", "p1.out", "p0.out", "v1.fwd", "p2.out", "p1.r1", "p0.own",
    "p0.r1", "p2.own", "v3.own1", "v2.fwd", "v2.own2", "gk.near", "v0.own1", "p2.r1", "p1.r2", "p0.r2",
    "gk.far", "c1.mm", "v3.fwd", "p2.r2", "p3.out", "p1.own1", "p3.own", "v3.own2", "p3.r1", "c1.r2", "p0.own1",
    "c2.mm", "p2.own1", "p1.fwd", "p3.r2", "v0.fwd", "c1.own1", "c2.r2", "p2.fwd", "v0.own2", "p2.own2",
    "c3.mm", "p1.own2", "p3.own1", "p3.own2", "c1.own2", "c1.fwd", "c2.own1", "p0.fwd", "c3.r2", "p2.km",
    "c0.mm", "p3.fwd", "c2.own2", "c1.t1", "p0.own2", "c2.fwd", "c0.r2", "p1.km", "p3.km", "c3.own1", "c2.t1",
    "c3.own2", "c1.tn", "p0.km", "c1.t2", "c2.tn", "c3.fwd", "c0.own1", "c2.to", "c3.t1", "c0.fwd", "c0.own2",
    "c3.tn", "c2.t2", "c1.to", "c3.to", "c0.t1", "c0.to", "c1.fin", "c3.t2", "c0.tn", "c2.fin", "c0.t2",
    "c3.fin", "c0.fin",
)


def at_multiple(index, size, step=None):
    return pl.ds(pl.multiple_of(index * (step or size), step or size), size)


def dot(a, b):
    return jnp.dot(a, b, preferred_element_type=F32)


def kernel(
    a_ref, g_ref, u_ref, v_ref, o_ref,
    a_all, u_all, g_all, v_all,
    act_out, act_in, act_part, act_s1, act_r1, act_s2, act_r2, act_t,
    grad_part, grad_s1, grad_r1, grad_s2, grad_r2, grad_rot,
    tile_part, tile_s1, tile_r1, tile_s2, tile_r2,
    send_sem, recv_sem, local_sem,
):
    row, col = lax.axis_index("row"), lax.axis_index("col")
    y, x = lax.div(row, 4), lax.rem(row, 4)
    z, core = lax.div(col, 2), lax.rem(col, 2)
    mate = 1 - core

    def step(position, by):
        return lax.rem(position + by, 4)

    def device(y, x, z, core):
        return (y * 4 + x, z * 2 + core)

    x_ring = (device(y, step(x, 1), z, core), device(y, step(x, 3), z, core))
    y_ring = (device(step(y, 1), x, z, core), device(step(y, 3), x, z, core))
    z_ring = (device(y, x, step(z, 1), core), device(y, x, step(z, 3), core))
    x_far = device(y, step(x, 2), z, core)
    other = device(y, x, z, mate)

    local = []

    def keep(src, dst):
        copy = pltpu.make_async_copy(src, dst, local_sem.at[len(local)])
        copy.start()
        local.append(copy)
        return copy

    own_rows = pl.multiple_of(z * 256 + core * 128, 128)
    x_lanes = at_multiple(x, 512)
    g_keep = keep(g_ref.at[at_multiple(x, 128)], g_all.at[pl.ds(own_rows, 128), x_lanes])
    act_keeps = [
        keep(a_ref, a_all.at[at_multiple(x, 256)]),
        keep(u_ref.at[:, pl.ds(0, 256)], u_all.at[y * 2]),
        keep(u_ref.at[:, pl.ds(256, 256)], u_all.at[y * 2 + 1]),
    ]
    v_keeps = [
        keep(v_ref.at[:, pl.ds(c * WIDTH, WIDTH)], v_all.at[c, at_multiple(x, 512)]) for c in range(CHUNKS)
    ]

    partners = (*x_ring, *y_ring, *z_ring, x_far, other)
    barrier = pltpu.get_barrier_semaphore()
    for partner in partners:
        pl.semaphore_signal(barrier, inc=1, device_id=partner, device_id_type=MESH)
    pl.semaphore_wait(barrier, len(partners))

    sent, arrived = [], set()

    def send(src, dst, target):
        index = len(sent)
        copy = pltpu.make_async_remote_copy(
            src_ref=src, dst_ref=dst,
            send_sem=send_sem.at[index], recv_sem=recv_sem.at[index],
            device_id=target, device_id_type=MESH,
        )
        copy.start()
        sent.append(copy)
        return copy

    def arrive(*copies):
        for copy in copies:
            if id(copy) not in arrived:
                arrived.add(id(copy))
                copy.wait_recv()

    def landed(*copies):
        for copy in copies:
            if id(copy) not in arrived:
                arrived.add(id(copy))
                copy.wait()

    steps = {}

    class Gather:
        def __init__(self, name, slot, position, ring, own=None, ready=lambda: None):
            self.own = own or (lambda half: slot(position, half))
            self.slot, self.position, self.ring, self.ready = slot, position, ring, ready
            steps[name + ".own1"] = self.first
            steps[name + ".own2"] = self.second
            steps[name + ".fwd"] = self.forward

        def first(self):
            self.ready()
            right, left = self.ring
            self.r0 = send(self.own(0), self.slot(self.position, 0), right)
            self.l1 = send(self.own(1), self.slot(self.position, 1), left)

        def second(self):
            right, left = self.ring
            self.r1 = send(self.own(1), self.slot(self.position, 1), right)
            self.l0 = send(self.own(0), self.slot(self.position, 0), left)

        def forward(self):
            right, left = self.ring
            arrive(self.r0)
            before = self.slot(step(self.position, 3), 0)
            self.rr = send(before, before, right)
            arrive(self.l1)
            after = self.slot(step(self.position, 1), 1)
            self.ll = send(after, after, left)

        def early(self):
            arrive(self.r0, self.l1)

        def near(self):
            arrive(self.r0, self.l1, self.r1, self.l0)

        def far(self):
            arrive(self.rr, self.ll)

    class Reduce:
        def __init__(self, part, half, ring, s1, r1, s2, r2):
            self.part, self.half, self.ring = part, half, ring
            self.s1, self.r1, self.s2, self.r2 = s1, r1, s2, r2

        def first(self):
            right, left = self.ring
            block = self.part(2)
            self.s1[0] = block[:self.half].astype(BF16)
            self.s1[1] = block[self.half:].astype(BF16)
            self.right1 = send(self.s1.at[0], self.r1.at[0], right)
            self.left1 = send(self.s1.at[1], self.r1.at[1], left)

        def second(self):
            right, left = self.ring
            half = self.half
            block = self.part(1)
            arrive(self.right1)
            self.s2[0, :half] = (block[:half] + self.r1[0].astype(F32)).astype(BF16)
            self.s2[0, half:] = block[half:].astype(BF16)
            self.right2 = send(self.s2.at[0], self.r2.at[0], right)
            block = self.part(3)
            arrive(self.left1)
            self.s2[1, :half] = block[:half].astype(BF16)
            self.s2[1, half:] = (block[half:] + self.r1[1].astype(F32)).astype(BF16)
            self.left2 = send(self.s2.at[1], self.r2.at[1], left)

        def last(self):
            block = self.part(0)
            arrive(self.right2, self.left2)
            return block + self.r2[0].astype(F32) + self.r2[1].astype(F32)

    swaps = []

    def g_swap():
        for by, target in ((1, x_ring[0]), (3, x_ring[1]), (2, x_far)):
            swaps.append(send(
                g_ref.at[at_multiple(step(x, by), 128)],
                g_all.at[pl.ds(own_rows, 128), x_lanes], target))

    def g_swapped():
        landed(g_keep)
        arrive(*swaps)

    steps["ga"] = g_swap
    g_gather = Gather(
        "g", lambda p, half: g_all.at[pl.ds(pl.multiple_of(p * 256 + core * 128 + half * 64, 64), 64)],
        z, z_ring, ready=g_swapped)
    g_mates = []

    def g_mate(*offsets):
        for by in offsets:
            block = g_all.at[pl.ds(pl.multiple_of(step(z, by) * 256 + core * 128, 128), 128)]
            g_mates.append(send(block, block, other))

    def g_mate_own():
        g_swapped()
        g_mate(0)

    def g_mate_near():
        g_gather.near()
        g_mate(1, 3)

    def g_mate_far():
        g_gather.far()
        g_mate(2)

    steps["gk.own"], steps["gk.near"], steps["gk.far"] = g_mate_own, g_mate_near, g_mate_far

    def g_done():
        g_gather.near()
        g_gather.far()
        arrive(*g_mates)

    u_gather = Gather(
        "u", lambda p, half: u_all.at[p * 2 + half], y, y_ring,
        own=lambda half: u_ref.at[:, pl.ds(half * 256, 256)])
    a_gather = Gather(
        "a", lambda p, half: a_all.at[pl.ds(pl.multiple_of(p * 256 + half * 128, 128), 128)], x, x_ring,
        own=lambda half: a_ref.at[pl.ds(half * 128, 128)])
    v_gathers = [
        Gather(
            f"v{c}",
            lambda p, half, c=c: v_all.at[c, pl.ds(pl.multiple_of(p * 512 + half * 256, 256), 256)], x, x_ring,
            own=lambda half, c=c: v_ref.at[pl.ds(half * 256, 256), pl.ds(c * WIDTH, WIDTH)])
        for c in range(CHUNKS)
    ]

    first_block, second_block = step(y, 3 - 2 * core), step(y, 1 + 2 * core)
    stages = (
        (y, y, lambda: None),
        (first_block, second_block, u_gather.early),
        (step(y, 2), step(y, 2), u_gather.far),
        (second_block, first_block, u_gather.near),
    )

    class Piece:
        def __init__(self, s):
            self.s = s
            self.own_block, self.mate_block, self.ready = stages[s]
            self.rows = pl.multiple_of(self.own_block * 512 + core * 256, 256)
            self.reduce = Reduce(
                self.part, 128, z_ring, act_s1.at[s], act_r1.at[s], act_s2.at[s], act_r2.at[s])
            name = f"p{s}"
            steps[name + ".out"], steps[name + ".own"] = self.out, self.own
            steps[name + ".r1"], steps[name + ".r2"] = self.first, self.reduce.second
            self.gather = Gather(
                name,
                lambda p, half: act_t.at[
                    pl.ds(pl.multiple_of(self.rows + half * 128, 128), 128), at_multiple(p, 256)],
                z, z_ring, ready=self.total)
            steps[name + ".km"] = self.finish

        def inputs(self):
            landed(*act_keeps)
            a_gather.near()
            a_gather.far()
            self.ready()

        def out(self):
            self.inputs()

            @pl.loop(0, 2)
            def _(m):
                rows = at_multiple(m, 512)
                act_out[self.s, rows] = dot(a_all[rows], u_all[self.mate_block * 2 + mate]).astype(BF16)

            self.swap = send(act_out.at[self.s], act_in.at[self.s], other)

        def own(self):
            self.inputs()

            @pl.loop(0, 2)
            def _(m):
                rows = at_multiple(m, 512)
                act_part[self.s, rows] = dot(a_all[rows], u_all[self.own_block * 2 + core])

        def part(self, by):
            rows = at_multiple(step(z, by), 256)
            return act_part[self.s, rows] + act_in[self.s, rows].astype(F32)

        def first(self):
            arrive(self.swap)
            self.reduce.first()

        def total(self):
            act_t[pl.ds(self.rows, 256), at_multiple(z, 256)] = self.reduce.last().T.astype(BF16)

        def finish(self):
            self.gather.near()
            self.gather.far()
            piece = act_t.at[pl.ds(self.rows, 256)]
            self.mates = send(piece, piece, other)

        def done(self):
            self.gather.near()
            self.gather.far()
            arrive(self.mates)

    pieces = [Piece(s) for s in range(4)]

    class Chunk:
        def __init__(self, c):
            self.c = c
            self.lanes = pl.ds(c * WIDTH, WIDTH)
            self.reduce = Reduce(
                lambda by: grad_part[c, at_multiple(step(y, by), 256)], 128, y_ring,
                grad_s1.at[c], grad_r1.at[c], grad_s2.at[c], grad_r2.at[c])
            self.out = Reduce(
                self.product, 256, y_ring, tile_s1.at[c], tile_r1.at[c], tile_s2.at[c], tile_r2.at[c])
            name = f"c{c}"
            steps[name + ".mm"], steps[name + ".r2"] = self.multiply, self.reduce.second
            self.gather = Gather(
                name, lambda p, half: grad_rot.at[c, half, at_multiple(p, 128)], x, x_ring, ready=self.total)
            steps[name + ".t1"], steps[name + ".tn"] = self.out.first, self.near_tiles
            steps[name + ".t2"], steps[name + ".to"] = self.out.second, self.own_tile
            steps[name + ".fin"] = self.finish

        def multiply(self):
            g_done()
            landed(v_keeps[self.c])
            v_gathers[self.c].near()
            v_gathers[self.c].far()

            @pl.loop(0, 2)
            def _(m):
                rows = at_multiple(m, 512)
                grad_part[self.c, rows] = dot(g_all[rows], v_all[self.c])

            self.reduce.first()

        def total(self):
            total = self.reduce.last().astype(BF16)
            rows = at_multiple(x, 128)
            grad_rot[self.c, 0, rows] = total[:128]
            grad_rot[self.c, 1, rows] = total[128:]

        def tile(self, t, *needs):
            self.gather.near()
            self.gather.far()
            for piece in needs:
                piece.done()
            product = dot(act_t[at_multiple(t, 512)], grad_rot[self.c].reshape(1024, WIDTH))
            return product * product

        def product(self, by):
            if by == 2:
                return self.tile(step(y, 2), pieces[2])
            if by == 0:
                return o_ref[:, self.lanes]
            return tile_part[self.c, by // 2]

        def near_tiles(self):
            for i, by in enumerate((1, 3)):
                tile_part[self.c, i] = self.tile(step(y, by), pieces[1], pieces[3])

        def own_tile(self):
            o_ref[:, self.lanes] = self.tile(y, pieces[0])

        def finish(self):
            o_ref[:, self.lanes] = self.out.last() * (1.0 / (SEQS * SEQ_LEN))

    chunks = [Chunk(c) for c in range(CHUNKS)]
    for name in ORDER:
        steps[name]()
    for copy in sent:
        copy.wait_send()


def shards(activations, out_grads, input_basis, output_basis):
    hbm = pl.BlockSpec(memory_space=pl.ANY)
    vmem = pl.BlockSpec(memory_space=pltpu.VMEM)

    def bf16(*sizes):
        return pltpu.VMEM(sizes, BF16)

    def f32(*sizes):
        return pltpu.VMEM(sizes, F32)

    return pl.pallas_call(
        kernel,
        out_shape=jax.ShapeDtypeStruct((512, 1024), F32),
        in_specs=[hbm] * 4,
        out_specs=vmem,
        scratch_shapes=[
            bf16(1024, 1024), bf16(8, 1024, 256), bf16(1024, 2048), bf16(CHUNKS, 2048, WIDTH),
            bf16(4, 1024, 256), bf16(4, 1024, 256), f32(4, 1024, 256),
            bf16(4, 2, 128, 256), bf16(4, 2, 128, 256), bf16(4, 2, 256, 256), bf16(4, 2, 256, 256),
            bf16(2048, 1024),
            f32(CHUNKS, 1024, WIDTH),
            bf16(CHUNKS, 2, 128, WIDTH), bf16(CHUNKS, 2, 128, WIDTH),
            bf16(CHUNKS, 2, 256, WIDTH), bf16(CHUNKS, 2, 256, WIDTH), bf16(CHUNKS, 2, 512, WIDTH),
            f32(CHUNKS, 2, 512, WIDTH),
            bf16(CHUNKS, 2, 256, WIDTH), bf16(CHUNKS, 2, 256, WIDTH),
            bf16(CHUNKS, 2, 512, WIDTH), bf16(CHUNKS, 2, 512, WIDTH),
            pltpu.SemaphoreType.DMA((N_SEM,)), pltpu.SemaphoreType.DMA((N_SEM,)),
            pltpu.SemaphoreType.DMA((4 + CHUNKS,)),
        ],
        compiler_params=pltpu.CompilerParams(
            collective_id=0, has_side_effects=True, vmem_limit_bytes=60 * 2**20),
        cost_estimate=pl.CostEstimate(flops=13 * 10**9, bytes_accessed=5 * 2**20, transcendentals=0),
    )(activations, out_grads, input_basis, output_basis)


def solution(mesh):
    return jax.shard_map(
        shards,
        mesh=mesh,
        in_specs=(P("row", "col"), P("col", "row"), P("col", "row"), P("row", "col")),
        out_specs=P("row", "col"),
        check_vma=False,
    )
```

```python
import jax
import jax.numpy as jnp
from jax import lax
from jax.experimental import pallas as pl
from jax.experimental.pallas import tpu as pltpu
from jax.sharding import PartitionSpec as P

SEQS = 4
SEQ_LEN = 1024
MESH = pl.DeviceIdType.MESH
BF16 = jnp.bfloat16
F32 = jnp.float32
WIDTHS = (256, 256, 256, 256)
CHUNKS = len(WIDTHS)
LANES = [pl.ds(sum(WIDTHS[:c]), WIDTHS[c]) for c in range(CHUNKS)]
N_SEM = 120 + 24 * CHUNKS

ORDER = (
    "ga", "a.own1", "a.own2", "u.own1", "gk.own", "g.own1", "u.fwd", "a.fwd", "g.fwd", "v1.own1", "u.own2",
    "v2.own1", "g.own2", "v1.own2", "p1.own", "p1.out", "p0.out", "v1.fwd", "p2.out", "p1.r1", "p0.own",
    "p0.r1", "p2.own", "v3.own1", "v2.fwd", "v2.own2", "gk.near", "v0.own1", "p2.r1", "p1.r2", "p0.r2",
    "gk.far", "c1.mm", "v3.fwd", "p2.r2", "p3.out", "p1.own1", "p3.own", "v3.own2", "p3.r1", "c1.r2", "p0.own1",
    "c2.mm", "p2.own1", "p1.fwd", "p3.r2", "v0.fwd", "c1.own1", "c2.r2", "p2.fwd", "v0.own2", "p2.own2",
    "c3.mm", "p1.own2", "p3.own1", "p3.own2", "c1.own2", "c1.fwd", "c2.own1", "p0.fwd", "c3.r2", "p2.km",
    "c0.mm", "p3.fwd", "c2.own2", "c1.t1", "p0.own2", "c2.fwd", "c0.r2", "p1.km", "p3.km", "c3.own1", "c2.t1",
    "c3.own2", "c1.tn", "p0.km", "c1.t2", "c2.tn", "c3.fwd", "c0.own1", "c2.to", "c3.t1", "c0.fwd", "c0.own2",
    "c3.tn", "c2.t2", "c1.to", "c3.to", "c0.t1", "c0.to", "c1.fin", "c3.t2", "c0.tn", "c2.fin", "c0.t2",
    "c3.fin", "c0.fin",
)


def at_multiple(index, size, step=None):
    return pl.ds(pl.multiple_of(index * (step or size), step or size), size)


def dot(a, b):
    return jnp.dot(a, b, preferred_element_type=F32)


def kernel(
    a_ref, g_ref, u_ref, v_ref, o_ref,
    a_all, u_all, g_all, v_all,
    act_out, act_in, act_part, act_s1, act_r1, act_s2, act_r2, act_t,
    grad_part, grad_s1, grad_r1, grad_s2, grad_r2, grad_rot,
    tile_part, tile_s1, tile_r1, tile_s2, tile_r2, result,
    send_sem, recv_sem, local_sem,
):
    row, col = lax.axis_index("row"), lax.axis_index("col")
    y, x = lax.div(row, 4), lax.rem(row, 4)
    z, core = lax.div(col, 2), lax.rem(col, 2)
    mate = 1 - core

    def step(position, by):
        return lax.rem(position + by, 4)

    def device(y, x, z, core):
        return (y * 4 + x, z * 2 + core)

    x_ring = (device(y, step(x, 1), z, core), device(y, step(x, 3), z, core))
    y_ring = (device(step(y, 1), x, z, core), device(step(y, 3), x, z, core))
    z_ring = (device(y, x, step(z, 1), core), device(y, x, step(z, 3), core))
    x_far = device(y, step(x, 2), z, core)
    other = device(y, x, z, mate)

    local = []

    def keep(src, dst):
        copy = pltpu.make_async_copy(src, dst, local_sem.at[len(local)])
        copy.start()
        local.append(copy)
        return copy

    own_rows = pl.multiple_of(z * 256 + core * 128, 128)
    x_lanes = at_multiple(x, 512)
    g_keep = keep(g_ref.at[at_multiple(x, 128)], g_all.at[pl.ds(own_rows, 128), x_lanes])
    act_keeps = [
        keep(a_ref, a_all.at[at_multiple(x, 256)]),
        keep(u_ref.at[:, pl.ds(0, 256)], u_all.at[y * 2]),
        keep(u_ref.at[:, pl.ds(256, 256)], u_all.at[y * 2 + 1]),
    ]
    v_keeps = [
        keep(v_ref.at[:, lanes], v_all.at[at_multiple(x, 512), lanes]) for lanes in LANES
    ]

    partners = (*x_ring, *y_ring, *z_ring, x_far, other)
    barrier = pltpu.get_barrier_semaphore()
    for partner in partners:
        pl.semaphore_signal(barrier, inc=1, device_id=partner, device_id_type=MESH)
    pl.semaphore_wait(barrier, len(partners))

    sent, arrived = [], set()

    def send(src, dst, target):
        index = len(sent)
        copy = pltpu.make_async_remote_copy(
            src_ref=src, dst_ref=dst,
            send_sem=send_sem.at[index], recv_sem=recv_sem.at[index],
            device_id=target, device_id_type=MESH,
        )
        copy.start()
        sent.append(copy)
        return copy

    def arrive(*copies):
        for copy in copies:
            if id(copy) not in arrived:
                arrived.add(id(copy))
                copy.wait_recv()

    def landed(*copies):
        for copy in copies:
            if id(copy) not in arrived:
                arrived.add(id(copy))
                copy.wait()

    steps = {}

    class Gather:
        def __init__(self, name, slot, position, ring, own=None, ready=lambda: None):
            self.own = own or (lambda half: slot(position, half))
            self.slot, self.position, self.ring, self.ready = slot, position, ring, ready
            steps[name + ".own1"] = self.first
            steps[name + ".own2"] = self.second
            steps[name + ".fwd"] = self.forward

        def first(self):
            self.ready()
            right, left = self.ring
            self.r0 = send(self.own(0), self.slot(self.position, 0), right)
            self.l1 = send(self.own(1), self.slot(self.position, 1), left)

        def second(self):
            right, left = self.ring
            self.r1 = send(self.own(1), self.slot(self.position, 1), right)
            self.l0 = send(self.own(0), self.slot(self.position, 0), left)

        def forward(self):
            right, left = self.ring
            arrive(self.r0)
            before = self.slot(step(self.position, 3), 0)
            self.rr = send(before, before, right)
            arrive(self.l1)
            after = self.slot(step(self.position, 1), 1)
            self.ll = send(after, after, left)

        def early(self):
            arrive(self.r0, self.l1)

        def near(self):
            arrive(self.r0, self.l1, self.r1, self.l0)

        def far(self):
            arrive(self.rr, self.ll)

    class Reduce:
        def __init__(self, part, half, ring, s1, r1, s2, r2):
            self.part, self.half, self.ring = part, half, ring
            self.s1, self.r1, self.s2, self.r2 = s1, r1, s2, r2

        def first(self):
            right, left = self.ring
            block = self.part(2)
            self.s1[0] = block[:self.half].astype(BF16)
            self.s1[1] = block[self.half:].astype(BF16)
            self.right1 = send(self.s1.at[0], self.r1.at[0], right)
            self.left1 = send(self.s1.at[1], self.r1.at[1], left)

        def second(self):
            right, left = self.ring
            half = self.half
            block = self.part(1)
            arrive(self.right1)
            self.s2[0, :half] = (block[:half] + self.r1[0].astype(F32)).astype(BF16)
            self.s2[0, half:] = block[half:].astype(BF16)
            self.right2 = send(self.s2.at[0], self.r2.at[0], right)
            block = self.part(3)
            arrive(self.left1)
            self.s2[1, :half] = block[:half].astype(BF16)
            self.s2[1, half:] = (block[half:] + self.r1[1].astype(F32)).astype(BF16)
            self.left2 = send(self.s2.at[1], self.r2.at[1], left)

        def last(self):
            block = self.part(0)
            arrive(self.right2, self.left2)
            return block + self.r2[0].astype(F32) + self.r2[1].astype(F32)

    swaps = []

    def g_swap():
        for by, target in ((1, x_ring[0]), (3, x_ring[1]), (2, x_far)):
            swaps.append(send(
                g_ref.at[at_multiple(step(x, by), 128)],
                g_all.at[pl.ds(own_rows, 128), x_lanes], target))

    def g_swapped():
        landed(g_keep)
        arrive(*swaps)

    steps["ga"] = g_swap
    g_gather = Gather(
        "g", lambda p, half: g_all.at[pl.ds(pl.multiple_of(p * 256 + core * 128 + half * 64, 64), 64)],
        z, z_ring, ready=g_swapped)
    g_mates = []

    def g_mate(*offsets):
        for by in offsets:
            block = g_all.at[pl.ds(pl.multiple_of(step(z, by) * 256 + core * 128, 128), 128)]
            g_mates.append(send(block, block, other))

    def g_mate_own():
        g_swapped()
        g_mate(0)

    def g_mate_near():
        g_gather.near()
        g_mate(1, 3)

    def g_mate_far():
        g_gather.far()
        g_mate(2)

    steps["gk.own"], steps["gk.near"], steps["gk.far"] = g_mate_own, g_mate_near, g_mate_far

    def g_done():
        g_gather.near()
        g_gather.far()
        arrive(*g_mates)

    u_gather = Gather(
        "u", lambda p, half: u_all.at[p * 2 + half], y, y_ring,
        own=lambda half: u_ref.at[:, pl.ds(half * 256, 256)])
    a_gather = Gather(
        "a", lambda p, half: a_all.at[pl.ds(pl.multiple_of(p * 256 + half * 128, 128), 128)], x, x_ring,
        own=lambda half: a_ref.at[pl.ds(half * 128, 128)])
    v_gathers = [
        Gather(
            f"v{c}",
            lambda p, half, c=c: v_all.at[pl.ds(pl.multiple_of(p * 512 + half * 256, 256), 256), LANES[c]], x, x_ring,
            own=lambda half, c=c: v_ref.at[pl.ds(half * 256, 256), LANES[c]])
        for c in range(CHUNKS)
    ]

    first_block, second_block = step(y, 3 - 2 * core), step(y, 1 + 2 * core)
    stages = (
        (y, y, lambda: None),
        (first_block, second_block, u_gather.early),
        (step(y, 2), step(y, 2), u_gather.far),
        (second_block, first_block, u_gather.near),
    )

    class Piece:
        def __init__(self, s):
            self.s = s
            self.own_block, self.mate_block, self.ready = stages[s]
            self.rows = pl.multiple_of(self.own_block * 512 + core * 256, 256)
            self.reduce = Reduce(
                self.part, 128, z_ring, act_s1.at[s], act_r1.at[s], act_s2.at[s], act_r2.at[s])
            name = f"p{s}"
            steps[name + ".out"], steps[name + ".own"] = self.out, self.own
            steps[name + ".r1"], steps[name + ".r2"] = self.first, self.reduce.second
            self.gather = Gather(
                name,
                lambda p, half: act_t.at[
                    pl.ds(pl.multiple_of(self.rows + half * 128, 128), 128), at_multiple(p, 256)],
                z, z_ring, ready=self.total)
            steps[name + ".km"] = self.finish

        def inputs(self):
            landed(*act_keeps)
            a_gather.near()
            a_gather.far()
            self.ready()

        def out(self):
            self.inputs()

            @pl.loop(0, 2)
            def _(m):
                rows = at_multiple(m, 512)
                act_out[self.s, rows] = dot(a_all[rows], u_all[self.mate_block * 2 + mate]).astype(BF16)

            self.swap = send(act_out.at[self.s], act_in.at[self.s], other)

        def own(self):
            self.inputs()

            @pl.loop(0, 2)
            def _(m):
                rows = at_multiple(m, 512)
                act_part[self.s, rows] = dot(a_all[rows], u_all[self.own_block * 2 + core])

        def part(self, by):
            rows = at_multiple(step(z, by), 256)
            return act_part[self.s, rows] + act_in[self.s, rows].astype(F32)

        def first(self):
            arrive(self.swap)
            self.reduce.first()

        def total(self):
            act_t[pl.ds(self.rows, 256), at_multiple(z, 256)] = self.reduce.last().T.astype(BF16)

        def finish(self):
            self.gather.near()
            self.gather.far()
            piece = act_t.at[pl.ds(self.rows, 256)]
            self.mates = send(piece, piece, other)

        def done(self):
            self.gather.near()
            self.gather.far()
            arrive(self.mates)

    pieces = [Piece(s) for s in range(4)]

    class Chunk:
        def __init__(self, c):
            self.c = c
            self.lanes = lanes = LANES[c]
            self.reduce = Reduce(
                lambda by: grad_part[at_multiple(step(y, by), 256), lanes], 128, y_ring,
                *(ref.at[:, :, lanes] for ref in (grad_s1, grad_r1, grad_s2, grad_r2)))
            self.out = Reduce(
                self.product, 256, y_ring, *(ref.at[:, :, lanes] for ref in (tile_s1, tile_r1, tile_s2, tile_r2)))
            name = f"c{c}"
            steps[name + ".mm"], steps[name + ".r2"] = self.multiply, self.reduce.second
            self.gather = Gather(
                name, lambda p, half: grad_rot.at[half, at_multiple(p, 128), lanes], x, x_ring, ready=self.total)
            steps[name + ".t1"], steps[name + ".tn"] = self.out.first, self.near_tiles
            steps[name + ".t2"], steps[name + ".to"] = self.out.second, self.own_tile
            steps[name + ".fin"] = self.finish

        def multiply(self):
            g_done()
            landed(v_keeps[self.c])
            v_gathers[self.c].near()
            v_gathers[self.c].far()

            @pl.loop(0, 2)
            def _(m):
                rows = at_multiple(m, 512)
                grad_part[rows, self.lanes] = dot(g_all[rows], v_all[:, self.lanes])

            self.reduce.first()

        def total(self):
            total = self.reduce.last().astype(BF16)
            rows = at_multiple(x, 128)
            grad_rot[0, rows, self.lanes] = total[:128]
            grad_rot[1, rows, self.lanes] = total[128:]

        def tile(self, t, *needs):
            self.gather.near()
            self.gather.far()
            for piece in needs:
                piece.done()
            product = dot(act_t[at_multiple(t, 512)], grad_rot[:, :, self.lanes].reshape(1024, WIDTHS[self.c]))
            return product * product

        def product(self, by):
            if by == 2:
                return self.tile(step(y, 2), pieces[2])
            if by == 0:
                return tile_part[2, :, self.lanes]
            return tile_part[by // 2, :, self.lanes]

        def near_tiles(self):
            for i, by in enumerate((1, 3)):
                tile_part[i, :, self.lanes] = self.tile(step(y, by), pieces[1], pieces[3])

        def own_tile(self):
            tile_part[2, :, self.lanes] = self.tile(y, pieces[0])

        def finish(self):
            result[:, self.lanes] = (self.out.last() * (1.0 / (SEQS * SEQ_LEN))).astype(result.dtype)
            results.append(keep(result.at[:, self.lanes], o_ref.at[:, self.lanes]))

    results = []
    chunks = [Chunk(c) for c in range(CHUNKS)]
    for name in ORDER:
        steps[name]()
    for copy in sent:
        copy.wait_send()
    for copy in results:
        copy.wait()


def hand_out(in_ref, out_ref):
    out_ref[...] = in_ref[...]


def shards(activations, out_grads, input_basis, output_basis):
    hbm = pl.BlockSpec(memory_space=pl.ANY)

    def bf16(*sizes):
        return pltpu.VMEM(sizes, BF16)

    def f32(*sizes):
        return pltpu.VMEM(sizes, F32)

    correction = pl.pallas_call(
        kernel,
        out_shape=jax.ShapeDtypeStruct((512, 1024), F32),
        in_specs=[hbm] * 4,
        out_specs=hbm,
        scratch_shapes=[
            bf16(1024, 1024), bf16(8, 1024, 256), bf16(1024, 2048), bf16(2048, 1024),
            bf16(4, 1024, 256), bf16(4, 1024, 256), f32(4, 1024, 256),
            bf16(4, 2, 128, 256), bf16(4, 2, 128, 256), bf16(4, 2, 256, 256), bf16(4, 2, 256, 256),
            bf16(2048, 1024),
            f32(1024, 1024),
            bf16(2, 128, 1024), bf16(2, 128, 1024), bf16(2, 256, 1024), bf16(2, 256, 1024), bf16(2, 512, 1024),
            f32(3, 512, 1024),
            bf16(2, 256, 1024), bf16(2, 256, 1024), bf16(2, 512, 1024), bf16(2, 512, 1024),
            pltpu.VMEM((512, 1024), F32),
            pltpu.SemaphoreType.DMA((N_SEM,)), pltpu.SemaphoreType.DMA((N_SEM,)),
            pltpu.SemaphoreType.DMA((4 + 2 * CHUNKS,)),
        ],
        compiler_params=pltpu.CompilerParams(
            collective_id=0, has_side_effects=True, vmem_limit_bytes=60 * 2**20),
        cost_estimate=pl.CostEstimate(flops=13 * 10**9, bytes_accessed=5 * 2**20, transcendentals=0),
    )(activations, out_grads, input_basis, output_basis)
    half = pl.BlockSpec((256, 1024), lambda i: (i, 0))
    return pl.pallas_call(
        hand_out, grid=(2,), in_specs=[half], out_specs=half,
        out_shape=jax.ShapeDtypeStruct((512, 1024), F32),
    )(correction)


def solution(mesh):
    return jax.shard_map(
        shards,
        mesh=mesh,
        in_specs=(P("row", "col"), P("col", "row"), P("col", "row"), P("row", "col")),
        out_specs=P("row", "col"),
        check_vma=False,
    )
```

```python
import jax
import jax.numpy as jnp
from jax import lax
from jax.experimental import pallas as pl
from jax.experimental.pallas import tpu as pltpu
from jax.sharding import PartitionSpec as P

SEQS = 4
SEQ_LEN = 1024
MESH = pl.DeviceIdType.MESH
BF16 = jnp.bfloat16
F32 = jnp.float32
WIDTHS = (256, 256, 256, 256)
CHUNKS = len(WIDTHS)
LANES = [pl.ds(sum(WIDTHS[:c]), WIDTHS[c]) for c in range(CHUNKS)]
N_SEM = 120 + 24 * CHUNKS

ORDER = (
    "ga", "a.own1", "a.own2", "u.own1", "gk.own", "g.own1", "u.fwd", "a.fwd", "g.fwd", "v1.own1", "u.own2",
    "v2.own1", "g.own2", "v1.own2", "p1.own", "p1.out", "p0.out", "v1.fwd", "p2.out", "p1.r1", "p0.own",
    "p0.r1", "p2.own", "v3.own1", "v2.fwd", "v2.own2", "gk.near", "v0.own1", "p2.r1", "p1.r2", "p0.r2",
    "gk.far", "c1.mm", "v3.fwd", "p2.r2", "p3.out", "p1.own1", "p3.own", "v3.own2", "p3.r1", "c1.r2", "p0.own1",
    "c2.mm", "p2.own1", "p1.fwd", "p3.r2", "v0.fwd", "c1.own1", "c2.r2", "p2.fwd", "v0.own2", "p2.own2",
    "c3.mm", "p1.own2", "p3.own1", "p3.own2", "c1.own2", "c1.fwd", "c2.own1", "p0.fwd", "c3.r2", "p2.km",
    "c0.mm", "p3.fwd", "c2.own2", "c1.t1", "p0.own2", "c2.fwd", "c0.r2", "p1.km", "p3.km", "c3.own1", "c2.t1",
    "c3.own2", "c1.tn", "p0.km", "c1.t2", "c2.tn", "c3.fwd", "c0.own1", "c2.to", "c3.t1", "c0.fwd", "c0.own2",
    "c3.tn", "c2.t2", "c1.to", "c3.to", "c0.t1", "c0.to", "c1.fin", "c3.t2", "c0.tn", "c2.fin", "c0.t2",
    "c3.fin", "c0.fin",
)


def at_multiple(index, size, step=None):
    return pl.ds(pl.multiple_of(index * (step or size), step or size), size)


def dot(a, b):
    return jnp.dot(a, b, preferred_element_type=F32)


def kernel(
    a_ref, g_ref, u_ref, v_ref, o_ref,
    a_all, u_all, g_all, v_all,
    act_out, act_in, act_part, act_s1, act_r1, act_s2, act_r2, act_t,
    grad_part, grad_s1, grad_r1, grad_s2, grad_r2, grad_rot,
    tile_part, tile_s1, tile_r1, tile_s2, tile_r2, result,
    send_sem, recv_sem, local_sem,
):
    row, col = lax.axis_index("row"), lax.axis_index("col")
    y, x = lax.div(row, 4), lax.rem(row, 4)
    z, core = lax.div(col, 2), lax.rem(col, 2)
    mate = 1 - core

    def step(position, by):
        return lax.rem(position + by, 4)

    def device(y, x, z, core):
        return (y * 4 + x, z * 2 + core)

    x_ring = (device(y, step(x, 1), z, core), device(y, step(x, 3), z, core))
    y_ring = (device(step(y, 1), x, z, core), device(step(y, 3), x, z, core))
    z_ring = (device(y, x, step(z, 1), core), device(y, x, step(z, 3), core))
    x_far = device(y, step(x, 2), z, core)
    other = device(y, x, z, mate)

    partners = (*x_ring, *y_ring, *z_ring, x_far, other)
    barrier = pltpu.get_barrier_semaphore()
    for partner in partners:
        pl.semaphore_signal(barrier, inc=1, device_id=partner, device_id_type=MESH)

    local = []

    def keep(src, dst):
        copy = pltpu.make_async_copy(src, dst, local_sem.at[len(local)])
        copy.start()
        local.append(copy)
        return copy

    own_rows = pl.multiple_of(z * 256 + core * 128, 128)
    x_lanes = at_multiple(x, 512)
    g_keep = keep(g_ref.at[at_multiple(x, 128)], g_all.at[pl.ds(own_rows, 128), x_lanes])
    act_keeps = [
        keep(a_ref, a_all.at[at_multiple(x, 256)]),
        keep(u_ref.at[:, pl.ds(0, 256)], u_all.at[y * 2]),
        keep(u_ref.at[:, pl.ds(256, 256)], u_all.at[y * 2 + 1]),
    ]
    v_keeps = [
        keep(v_ref.at[:, lanes], v_all.at[at_multiple(x, 512), lanes]) for lanes in LANES
    ]

    pl.semaphore_wait(barrier, len(partners))

    sent, arrived = [], set()

    def send(src, dst, target):
        index = len(sent)
        copy = pltpu.make_async_remote_copy(
            src_ref=src, dst_ref=dst,
            send_sem=send_sem.at[index], recv_sem=recv_sem.at[index],
            device_id=target, device_id_type=MESH,
        )
        copy.start()
        sent.append(copy)
        return copy

    def arrive(*copies):
        for copy in copies:
            if id(copy) not in arrived:
                arrived.add(id(copy))
                copy.wait_recv()

    def landed(*copies):
        for copy in copies:
            if id(copy) not in arrived:
                arrived.add(id(copy))
                copy.wait()

    steps = {}

    class Gather:
        def __init__(self, name, slot, position, ring, own=None, ready=lambda: None):
            self.own = own or (lambda half: slot(position, half))
            self.slot, self.position, self.ring, self.ready = slot, position, ring, ready
            steps[name + ".own1"] = self.first
            steps[name + ".own2"] = self.second
            steps[name + ".fwd"] = self.forward

        def first(self):
            self.ready()
            right, left = self.ring
            self.r0 = send(self.own(0), self.slot(self.position, 0), right)
            self.l1 = send(self.own(1), self.slot(self.position, 1), left)

        def second(self):
            right, left = self.ring
            self.r1 = send(self.own(1), self.slot(self.position, 1), right)
            self.l0 = send(self.own(0), self.slot(self.position, 0), left)

        def forward(self):
            right, left = self.ring
            arrive(self.r0)
            before = self.slot(step(self.position, 3), 0)
            self.rr = send(before, before, right)
            arrive(self.l1)
            after = self.slot(step(self.position, 1), 1)
            self.ll = send(after, after, left)

        def early(self):
            arrive(self.r0, self.l1)

        def near(self):
            arrive(self.r0, self.l1, self.r1, self.l0)

        def far(self):
            arrive(self.rr, self.ll)

    class Reduce:
        def __init__(self, part, half, ring, s1, r1, s2, r2):
            self.part, self.half, self.ring = part, half, ring
            self.s1, self.r1, self.s2, self.r2 = s1, r1, s2, r2

        def first(self):
            right, left = self.ring
            block = self.part(2)
            self.s1[0] = block[:self.half].astype(BF16)
            self.s1[1] = block[self.half:].astype(BF16)
            self.right1 = send(self.s1.at[0], self.r1.at[0], right)
            self.left1 = send(self.s1.at[1], self.r1.at[1], left)

        def second(self):
            right, left = self.ring
            half = self.half
            block = self.part(1)
            arrive(self.right1)
            self.s2[0, :half] = (block[:half] + self.r1[0].astype(F32)).astype(BF16)
            self.s2[0, half:] = block[half:].astype(BF16)
            self.right2 = send(self.s2.at[0], self.r2.at[0], right)
            block = self.part(3)
            arrive(self.left1)
            self.s2[1, :half] = block[:half].astype(BF16)
            self.s2[1, half:] = (block[half:] + self.r1[1].astype(F32)).astype(BF16)
            self.left2 = send(self.s2.at[1], self.r2.at[1], left)

        def last(self):
            block = self.part(0)
            arrive(self.right2, self.left2)
            return block + self.r2[0].astype(F32) + self.r2[1].astype(F32)

    swaps = []

    def g_swap():
        for by, target in ((1, x_ring[0]), (3, x_ring[1]), (2, x_far)):
            swaps.append(send(
                g_ref.at[at_multiple(step(x, by), 128)],
                g_all.at[pl.ds(own_rows, 128), x_lanes], target))

    def g_swapped():
        landed(g_keep)
        arrive(*swaps)

    steps["ga"] = g_swap
    g_gather = Gather(
        "g", lambda p, half: g_all.at[pl.ds(pl.multiple_of(p * 256 + core * 128 + half * 64, 64), 64)],
        z, z_ring, ready=g_swapped)
    g_mates = []

    def g_mate(*offsets):
        for by in offsets:
            block = g_all.at[pl.ds(pl.multiple_of(step(z, by) * 256 + core * 128, 128), 128)]
            g_mates.append(send(block, block, other))

    def g_mate_own():
        g_swapped()
        g_mate(0)

    def g_mate_near():
        g_gather.near()
        g_mate(1, 3)

    def g_mate_far():
        g_gather.far()
        g_mate(2)

    steps["gk.own"], steps["gk.near"], steps["gk.far"] = g_mate_own, g_mate_near, g_mate_far

    def g_done():
        g_gather.near()
        g_gather.far()
        arrive(*g_mates)

    u_gather = Gather(
        "u", lambda p, half: u_all.at[p * 2 + half], y, y_ring,
        own=lambda half: u_ref.at[:, pl.ds(half * 256, 256)])
    a_gather = Gather(
        "a", lambda p, half: a_all.at[pl.ds(pl.multiple_of(p * 256 + half * 128, 128), 128)], x, x_ring,
        own=lambda half: a_ref.at[pl.ds(half * 128, 128)])
    v_gathers = [
        Gather(
            f"v{c}",
            lambda p, half, c=c: v_all.at[pl.ds(pl.multiple_of(p * 512 + half * 256, 256), 256), LANES[c]], x, x_ring,
            own=lambda half, c=c: v_ref.at[pl.ds(half * 256, 256), LANES[c]])
        for c in range(CHUNKS)
    ]

    first_block, second_block = step(y, 3 - 2 * core), step(y, 1 + 2 * core)
    stages = (
        (y, y, lambda: None),
        (first_block, second_block, u_gather.early),
        (step(y, 2), step(y, 2), u_gather.far),
        (second_block, first_block, u_gather.near),
    )

    class Piece:
        def __init__(self, s):
            self.s = s
            self.own_block, self.mate_block, self.ready = stages[s]
            self.rows = pl.multiple_of(self.own_block * 512 + core * 256, 256)
            self.reduce = Reduce(
                self.part, 128, z_ring, act_s1.at[s], act_r1.at[s], act_s2.at[s], act_r2.at[s])
            name = f"p{s}"
            steps[name + ".out"], steps[name + ".own"] = self.out, self.own
            steps[name + ".r1"], steps[name + ".r2"] = self.first, self.reduce.second
            self.gather = Gather(
                name,
                lambda p, half: act_t.at[
                    pl.ds(pl.multiple_of(self.rows + half * 128, 128), 128), at_multiple(p, 256)],
                z, z_ring, ready=self.total)
            steps[name + ".km"] = self.finish

        def inputs(self):
            landed(*act_keeps)
            a_gather.near()
            a_gather.far()
            self.ready()

        def out(self):
            self.inputs()

            @pl.loop(0, 2)
            def _(m):
                rows = at_multiple(m, 512)
                act_out[self.s, rows] = dot(a_all[rows], u_all[self.mate_block * 2 + mate]).astype(BF16)

            self.swap = send(act_out.at[self.s], act_in.at[self.s], other)

        def own(self):
            self.inputs()

            @pl.loop(0, 2)
            def _(m):
                rows = at_multiple(m, 512)
                act_part[self.s, rows] = dot(a_all[rows], u_all[self.own_block * 2 + core])

        def part(self, by):
            rows = at_multiple(step(z, by), 256)
            return act_part[self.s, rows] + act_in[self.s, rows].astype(F32)

        def first(self):
            arrive(self.swap)
            self.reduce.first()

        def total(self):
            act_t[pl.ds(self.rows, 256), at_multiple(z, 256)] = self.reduce.last().T.astype(BF16)

        def finish(self):
            self.gather.near()
            self.gather.far()
            piece = act_t.at[pl.ds(self.rows, 256)]
            self.mates = send(piece, piece, other)

        def done(self):
            self.gather.near()
            self.gather.far()
            arrive(self.mates)

    pieces = [Piece(s) for s in range(4)]

    class Chunk:
        def __init__(self, c):
            self.c = c
            self.lanes = lanes = LANES[c]
            self.reduce = Reduce(
                lambda by: grad_part[at_multiple(step(y, by), 256), lanes], 128, y_ring,
                *(ref.at[:, :, lanes] for ref in (grad_s1, grad_r1, grad_s2, grad_r2)))
            self.out = Reduce(
                self.product, 256, y_ring, *(ref.at[:, :, lanes] for ref in (tile_s1, tile_r1, tile_s2, tile_r2)))
            name = f"c{c}"
            steps[name + ".mm"], steps[name + ".r2"] = self.multiply, self.reduce.second
            self.gather = Gather(
                name, lambda p, half: grad_rot.at[half, at_multiple(p, 128), lanes], x, x_ring, ready=self.total)
            steps[name + ".t1"], steps[name + ".tn"] = self.out.first, self.near_tiles
            steps[name + ".t2"], steps[name + ".to"] = self.out.second, self.own_tile
            steps[name + ".fin"] = self.finish

        def multiply(self):
            g_done()
            landed(v_keeps[self.c])
            v_gathers[self.c].near()
            v_gathers[self.c].far()

            @pl.loop(0, 2)
            def _(m):
                rows = at_multiple(m, 512)
                grad_part[rows, self.lanes] = dot(g_all[rows], v_all[:, self.lanes])

            self.reduce.first()

        def total(self):
            total = self.reduce.last().astype(BF16)
            rows = at_multiple(x, 128)
            grad_rot[0, rows, self.lanes] = total[:128]
            grad_rot[1, rows, self.lanes] = total[128:]

        def tile(self, t, *needs):
            self.gather.near()
            self.gather.far()
            for piece in needs:
                piece.done()
            product = dot(act_t[at_multiple(t, 512)], grad_rot[:, :, self.lanes].reshape(1024, WIDTHS[self.c]))
            return product * product

        def product(self, by):
            if by == 2:
                return self.tile(step(y, 2), pieces[2])
            if by == 0:
                return tile_part[2, :, self.lanes]
            return tile_part[by // 2, :, self.lanes]

        def near_tiles(self):
            for i, by in enumerate((1, 3)):
                tile_part[i, :, self.lanes] = self.tile(step(y, by), pieces[1], pieces[3])

        def own_tile(self):
            tile_part[2, :, self.lanes] = self.tile(y, pieces[0])

        def finish(self):
            result[:, self.lanes] = (self.out.last() * (1.0 / (SEQS * SEQ_LEN))).astype(result.dtype)
            results.append(keep(result.at[:, self.lanes], o_ref.at[:, self.lanes]))

    results = []
    chunks = [Chunk(c) for c in range(CHUNKS)]
    for name in ORDER:
        steps[name]()
    for copy in sent:
        copy.wait_send()
    for copy in results:
        copy.wait()


def hand_out(in_ref, out_ref):
    out_ref[...] = in_ref[...]


def shards(activations, out_grads, input_basis, output_basis):
    hbm = pl.BlockSpec(memory_space=pl.ANY)

    def bf16(*sizes):
        return pltpu.VMEM(sizes, BF16)

    def f32(*sizes):
        return pltpu.VMEM(sizes, F32)

    correction = pl.pallas_call(
        kernel,
        out_shape=jax.ShapeDtypeStruct((512, 1024), F32),
        in_specs=[hbm] * 4,
        out_specs=hbm,
        scratch_shapes=[
            bf16(1024, 1024), bf16(8, 1024, 256), bf16(1024, 2048), bf16(2048, 1024),
            bf16(4, 1024, 256), bf16(4, 1024, 256), f32(4, 1024, 256),
            bf16(4, 2, 128, 256), bf16(4, 2, 128, 256), bf16(4, 2, 256, 256), bf16(4, 2, 256, 256),
            bf16(2048, 1024),
            f32(1024, 1024),
            bf16(2, 128, 1024), bf16(2, 128, 1024), bf16(2, 256, 1024), bf16(2, 256, 1024), bf16(2, 512, 1024),
            f32(3, 512, 1024),
            bf16(2, 256, 1024), bf16(2, 256, 1024), bf16(2, 512, 1024), bf16(2, 512, 1024),
            pltpu.VMEM((512, 1024), F32),
            pltpu.SemaphoreType.DMA((N_SEM,)), pltpu.SemaphoreType.DMA((N_SEM,)),
            pltpu.SemaphoreType.DMA((4 + 2 * CHUNKS,)),
        ],
        compiler_params=pltpu.CompilerParams(
            collective_id=0, has_side_effects=True, vmem_limit_bytes=60 * 2**20),
        cost_estimate=pl.CostEstimate(flops=13 * 10**9, bytes_accessed=5 * 2**20, transcendentals=0),
    )(activations, out_grads, input_basis, output_basis)
    half = pl.BlockSpec((256, 1024), lambda i: (i, 0))
    return pl.pallas_call(
        hand_out, grid=(2,), in_specs=[half], out_specs=half,
        out_shape=jax.ShapeDtypeStruct((512, 1024), F32),
    )(correction)


def solution(mesh):
    return jax.shard_map(
        shards,
        mesh=mesh,
        in_specs=(P("row", "col"), P("col", "row"), P("col", "row"), P("row", "col")),
        out_specs=P("row", "col"),
        check_vma=False,
    )
```
